32 devices in a mesh: pts: 16 (over z, x, core), dir: 2 (over y).
Axes of the slice: x: 2, y: 2, z: 4, core: 2. Of those that a mesh axis runs over, the one named last changes fastest.
Arguments:
- action: float32 [50, 32, 256, 256], P(None, 'dir', 'pts'), may hold values from 0 to 60, as said below
- currents: float32 [2, 256, 256], P(None, 'pts'), may hold values from -0.1 to 0.1, as said below
- land_mask: int32 [256, 256], P('pts'), may hold values 0 or 1
- group_speed: float32 [50], replicated, may hold values from 0.02 to 0.55
- group_ratio: float32 [50], replicated, may hold values from 0.5 to 1
- bin_weight: float32 [50], replicated, may hold values from 0.002 to 0.02
Outputs:
- new_action: float32 [50, 32, 256, 256], P(None, 'dir', 'pts')
- wave_force: float32 [2, 256, 256], P(None, 'pts')
The draws below stay inside these ranges and needn't reach their ends.
Inputs may be any that keep to these rules, and one draw needn't show every extreme that they name: Positive action densities. currents vary slowly from point to point.
All inputs are finite; a program needn't handle non-finite values. No bound on the sum of `land_mask` on one device may be relied on, other than what follows from the above.
Results may differ from the reference program's by a relative error of at most 0.00022.
Values sent between devices are 32-bit elements; how exact they have to be, the bound alone decides.
A program may use at most 128 MiB of HBM per device.

```python
import math
import jax
import jax.numpy as jnp
from jax import lax

NF = 50
NDIR = 32
NY = 256
NX = 256


def draw_action(key, part):
    k_dir, k_rough, k_freq = jax.random.split(key, 3)
    center = jax.random.uniform(k_dir, (), jnp.float32, 1.2 * math.pi, 1.6 * math.pi)
    angles = jnp.arange(NDIR).astype(jnp.float32) * (2.0 * math.pi / NDIR)
    spread = jnp.exp(0.5 * jnp.cos(angles - center))
    roughness = jnp.exp(jax.random.uniform(k_rough, (NF, NDIR, NX, NY), jnp.float32, math.log(0.5), math.log(2.0)))
    levels = jnp.exp(jax.random.uniform(k_freq, (NF,), jnp.float32, -0.5, 0.5))
    return spread[None, :, None, None] * roughness * levels[:, None, None, None]


def draw_currents(key, part):
    k_wave, k_sign, k_phase, k_amp, k_rough = jax.random.split(key, 5)
    rows = jnp.arange(NX).astype(jnp.float32)[None, :, None]
    cols = jnp.arange(NY).astype(jnp.float32)[None, None, :]
    modes = 3
    wavelengths = jax.random.uniform(k_wave, (2, modes, 2), jnp.float32, 40.0, 80.0)
    signs = jnp.where(jax.random.uniform(k_sign, (2, modes, 2), jnp.float32) < 0.5, -1.0, 1.0)
    numbers = 2.0 * math.pi / wavelengths * signs
    phases = jax.random.uniform(k_phase, (2, modes), jnp.float32, 0.0, 2.0 * math.pi)
    amps = jax.random.uniform(k_amp, (2, modes), jnp.float32, 0.035, 0.05)
    rough_size = 0.002
    field = jnp.zeros((2, NX, NY), jnp.float32)
    for mode in range(modes):
        arg = numbers[:, mode, 0][:, None, None] * rows + numbers[:, mode, 1][:, None, None] * cols + phases[:, mode][:, None, None]
        field = field + amps[:, mode][:, None, None] * jnp.sin(arg)
    saturated = 0.095 * jnp.tanh(field / 0.05)
    rough = jax.random.uniform(k_rough, (2, NX, NY), jnp.float32, -rough_size, rough_size)
    return saturated + rough


def with_ends(values, own_key, smallest, high):
    place = [jax.random.randint(jax.random.fold_in(own_key, axis), (), 0, length) for axis, length in enumerate(values.shape)]
    longest = values.shape.index(max(values.shape))
    beside = place[:longest] + [(place[longest] + 1) % values.shape[longest]] + place[longest + 1:]
    return values.at[tuple(place)].set(smallest).at[tuple(beside)].set(high)


def setup_inputs(seed: int = 0) -> dict:
    key_of = jax.random.split(jax.random.key(seed), 7)
    action = draw_action(jax.random.fold_in(key_of[6], 71), 0)
    currents = draw_currents(jax.random.fold_in(key_of[6], 71), 0)
    land_mask = with_ends((jax.random.randint(key_of[2], (NX, NY), 0, 10) < 9).astype(jnp.int32), jax.random.fold_in(key_of[2], 1), 0, 1)
    group_speed = jnp.clip(jnp.exp(jax.random.uniform(key_of[3], (NF,), jnp.float32, math.log(0.02), math.log(0.55))), 0.02, 0.55)
    group_ratio = jnp.clip(jax.random.uniform(key_of[4], (NF,), jnp.float32, 0.5, 1.0), 0.5, 1.0)
    bin_weight = jnp.clip(jnp.exp(jax.random.uniform(key_of[5], (NF,), jnp.float32, math.log(0.002), math.log(0.02))), 0.002, 0.02)
    return dict(action=action, currents=currents, land_mask=land_mask, group_speed=group_speed, group_ratio=group_ratio, bin_weight=bin_weight)


def upwind(velocity, behind, in_front):
    return jnp.maximum(velocity, 0.0) * behind + jnp.minimum(velocity, 0.0) * in_front


def advance(extended, cur_u, cur_v, land_cells, cosine_terms, sine_terms, group_speed):
    speed_x = group_speed[:, None, None, None] * cosine_terms[None, :, None, None]
    speed_y = group_speed[:, None, None, None] * sine_terms[None, :, None, None]
    drift_x = speed_x + (0.5 * (cur_u[:-1] + cur_u[1:]))[None, None]
    flux_x = upwind(drift_x, extended[:, :, :-1], extended[:, :, 1:])
    middle = extended[:, :, 1:-1]
    side_v = jnp.pad(cur_v[1:-1], ((0, 0), (1, 1)))
    drift_y = speed_y + (0.5 * (side_v[:, :-1] + side_v[:, 1:]))[None, None]
    padded = jnp.pad(middle, ((0, 0), (0, 0), (0, 0), (1, 1)))
    flux_y = upwind(drift_y, padded[..., :-1], padded[..., 1:])
    change = (flux_x[:, :, 1:] - flux_x[:, :, :-1]) + (flux_y[..., 1:] - flux_y[..., :-1])
    return land_cells * (middle - change)


def row_slope(values):
    return 0.5 * (values[2:] - values[:-2])


def col_slope(values):
    padded = jnp.pad(values[1:-1], ((0, 0), (1, 1)))
    return 0.5 * (padded[:, 2:] - padded[:, :-2])


def shear_terms(ext_u, ext_v):
    return row_slope(ext_u), col_slope(ext_u), row_slope(ext_v), col_slope(ext_v)


def turn_rate(face_angles, shears, total_dirs):
    u_dx, u_dy, v_dx, v_dy = shears
    sines = jnp.sin(face_angles)[:, None, None]
    cosines = jnp.cos(face_angles)[:, None, None]
    scale = total_dirs / (2.0 * math.pi)
    return scale * (sines * cosines * (u_dx - v_dy) + sines * sines * u_dy - cosines * cosines * v_dx)


def refract(cycle_ext, turning):
    flux = upwind(turning[None], cycle_ext[:, :-1], cycle_ext[:, 1:])
    return cycle_ext[:, 1:-1] - (flux[:, 1:] - flux[:, :-1])


def stress_table(angles, bin_weight, group_ratio):
    cos_sq = (jnp.cos(angles) * jnp.cos(angles))[None]
    sin_sq = (jnp.sin(angles) * jnp.sin(angles))[None]
    cross = (jnp.sin(angles) * jnp.cos(angles))[None]
    ratio = group_ratio[:, None]
    weight = bin_weight[:, None]
    return jnp.stack([weight * (ratio * (1.0 + cos_sq) - 0.5), weight * ratio * cross, weight * (ratio * (1.0 + sin_sq) - 0.5)])


def wave_force_of(extended):
    first = -(row_slope(extended[0]) + col_slope(extended[1]))
    second = -(row_slope(extended[1]) + col_slope(extended[2]))
    return jnp.stack([first, second])


def reference(action, currents, land_mask, group_speed, group_ratio, bin_weight):
    land_cells = land_mask.astype(jnp.float32)
    step_angle = 2.0 * math.pi / NDIR
    angles = jnp.arange(NDIR).astype(jnp.float32) * step_angle
    ext_u = jnp.pad(currents[0], ((1, 1), (0, 0)))
    ext_v = jnp.pad(currents[1], ((1, 1), (0, 0)))
    shears = shear_terms(ext_u, ext_v)
    face_angles = (jnp.arange(NDIR + 1).astype(jnp.float32) - 0.5) * step_angle
    turning = turn_rate(face_angles, shears, NDIR)
    cosine_terms = jnp.cos(angles)
    sine_terms = jnp.sin(angles)

    def one_frequency(inputs):
        slab, speed = inputs
        spectra = land_cells * slab[None]
        for substep in range(2):
            extended = jnp.pad(spectra, ((0, 0), (0, 0), (1, 1), (0, 0)))
            spectra = advance(extended, ext_u, ext_v, land_cells, cosine_terms, sine_terms, speed[None])
        cycle_ext = jnp.concatenate([spectra[:, -1:], spectra, spectra[:, :1]], axis=1)
        return refract(cycle_ext, turning)[0]

    new_action = lax.map(one_frequency, (action, group_speed))
    stress = jnp.einsum("kfd,fdry->kry", stress_table(angles, bin_weight, group_ratio), new_action, precision=lax.Precision.HIGHEST)
    extended = jnp.pad(stress, ((0, 0), (1, 1), (0, 0)))
    return new_action, wave_force_of(extended)
```

```python
import functools
import math

import jax
import jax.numpy as jnp
from jax import lax
from jax.experimental import pallas as pl
from jax.experimental.pallas import tpu as pltpu
from jax.sharding import PartitionSpec as P

MESH = pl.DeviceIdType.MESH
LANES = 128
SUBS = 8
F32 = jnp.float32


def lane_of(shape):
    return lax.broadcasted_iota(jnp.int32, shape, 1)


def next_col(tiles):
    count = len(tiles)
    edge = lane_of(tiles[0].shape) == LANES - 1
    rolled = [pltpu.roll(t, LANES - 1, 1) for t in tiles]
    return [
        jnp.where(edge, rolled[c + 1] if c + 1 < count else 0.0, rolled[c])
        for c in range(count)
    ]


def prev_col(tiles, first):
    edge = lane_of(tiles[0].shape) == 0
    rolled = [pltpu.roll(t, 1, 1) for t in tiles]
    return [jnp.where(edge, rolled[c - 1] if c else first, rolled[c]) for c in range(len(tiles))]


def next_row(tiles, below):
    count = len(tiles)
    edge = lax.broadcasted_iota(jnp.int32, (SUBS, LANES), 0) == SUBS - 1
    rolled = [[pltpu.roll(t, SUBS - 1, 0) for t in row] for row in tiles]
    return [
        [
            jnp.where(edge, rolled[r + 1][c] if r + 1 < count else below[c], rolled[r][c])
            for c in range(len(below))
        ]
        for r in range(count)
    ]


def prev_row(tiles, above):
    edge = lax.broadcasted_iota(jnp.int32, (SUBS, LANES), 0) == 0
    rolled = [[pltpu.roll(t, 1, 0) for t in row] for row in tiles]
    return [
        [jnp.where(edge, rolled[r - 1][c] if r else above[c], rolled[r][c]) for c in range(len(above))]
        for r in range(len(tiles))
    ]


def split_cols(value):
    return [value[:, c * LANES:(c + 1) * LANES] for c in range(value.shape[1] // LANES)]


def load_tiles(ref, *lead):
    rows, cols = ref.shape[-2:]
    return [
        [
            ref[(*lead, pl.ds(r * SUBS, SUBS), pl.ds(c * LANES, LANES))]
            for c in range(cols // LANES)
        ]
        for r in range(rows // SUBS)
    ]


def load_row(ref, *lead):
    cols = ref.shape[-1]
    *head, row = lead
    return [ref[(*head, pl.ds(row, 1), pl.ds(c * LANES, LANES))] for c in range(cols // LANES)]


def store_tiles(ref, tiles, *lead):
    for r, row in enumerate(tiles):
        for c, tile in enumerate(row):
            ref[(*lead, pl.ds(r * SUBS, SUBS), pl.ds(c * LANES, LANES))] = tile


def pick(speed, behind, ahead):
    return speed * jnp.where(speed > 0.0, behind, ahead)


def transport_kernel(
    n_pts, n_dir, chunk,
    act, cur, land, gs, trig, cosb, sinb, face,
    a2, got, k_ref,
    buf, own_top, own_bot, halo_top, halo_bot, cur_top, cur_bot, land_top, land_bot,
    ub, vb, sea, rows, border, sel,
    in_sem, out_sem, up_send, up_recv, down_send, down_recv, cur_sem, dir_send, dir_recv,
):
    nf, nd, nr, nc = buf.shape
    chunks = nf // chunk
    ct = nc // LANES
    me = lax.axis_index("pts")
    mine = lax.axis_index("dir")
    has_prev = me > 0
    has_next = me < n_pts - 1
    before = jnp.maximum(me - 1, 0)
    after = jnp.minimum(me + 1, n_pts - 1)
    dir_after = lax.rem(mine + 1, n_dir)
    dir_before = lax.rem(mine + n_dir - 1, n_dir)

    def bring(c):
        part = pl.ds(c * chunk, chunk)
        return pltpu.make_async_copy(act.at[part], buf.at[part], in_sem.at[c])

    def put(c):
        part = pl.ds(c * chunk, chunk)
        return pltpu.make_async_copy(buf.at[part], a2.at[part], out_sem.at[c])

    def remote(src, dst, send, recv, where):
        return pltpu.make_async_remote_copy(
            src_ref=src, dst_ref=dst, send_sem=send, recv_sem=recv,
            device_id=where, device_id_type=MESH,
        )

    def up(c):
        part = pl.ds(c * chunk, chunk)
        return remote(own_top.at[part], halo_bot.at[part], up_send.at[c], up_recv.at[c], {"pts": before})

    def down(c):
        part = pl.ds(c * chunk, chunk)
        return remote(own_bot.at[part], halo_top.at[part], down_send.at[c], down_recv.at[c], {"pts": after})

    def cur_up():
        return remote(cur.at[:, pl.ds(0, SUBS)], cur_bot, cur_sem.at[0], cur_sem.at[1], {"pts": before})

    def cur_down():
        return remote(cur.at[:, pl.ds(nr - SUBS, SUBS)], cur_top, cur_sem.at[2], cur_sem.at[3], {"pts": after})

    def land_up():
        return remote(land.at[pl.ds(0, SUBS)], land_bot, cur_sem.at[4], cur_sem.at[5], {"pts": before})

    def land_down():
        return remote(land.at[pl.ds(nr - SUBS, SUBS)], land_top, cur_sem.at[6], cur_sem.at[7], {"pts": after})

    def turn(side, c):
        part = pl.ds(c * chunk, chunk)
        return remote(
            sel.at[side, part], got.at[side, part], dir_send.at[side, c], dir_recv.at[side, c],
            {"dir": dir_after if side == 0 else dir_before},
        )

    sides = sel.shape[0]

    def start_in(c, _):
        bring(c).start()
        return 0

    lax.fori_loop(0, chunks, start_in, 0)

    barrier = pltpu.get_barrier_semaphore()

    @pl.when(has_prev)
    def _():
        pl.semaphore_signal(barrier, inc=1, device_id={"pts": before}, device_id_type=MESH)

    @pl.when(has_next)
    def _():
        pl.semaphore_signal(barrier, inc=1, device_id={"pts": after}, device_id_type=MESH)

    pl.semaphore_signal(barrier, inc=1, device_id={"dir": dir_after}, device_id_type=MESH)
    if n_dir > 2:
        pl.semaphore_signal(barrier, inc=1, device_id={"dir": dir_before}, device_id_type=MESH)

    @pl.when(jnp.logical_not(has_prev))
    def _():
        def clear(f, _):
            halo_top[f] = jnp.zeros(halo_top.shape[1:], F32)
            return 0
        lax.fori_loop(0, nf, clear, 0)
        cur_top[...] = jnp.zeros(cur_top.shape, F32)
        land_top[...] = jnp.zeros(land_top.shape, jnp.int32)

    @pl.when(jnp.logical_not(has_next))
    def _():
        def clear(f, _):
            halo_bot[f] = jnp.zeros(halo_bot.shape[1:], F32)
            return 0
        lax.fori_loop(0, nf, clear, 0)
        cur_bot[...] = jnp.zeros(cur_bot.shape, F32)
        land_bot[...] = jnp.zeros(land_bot.shape, jnp.int32)

    others = has_prev.astype(jnp.int32) + has_next.astype(jnp.int32)
    pl.semaphore_wait(barrier, others + (2 if n_dir > 2 else 1))

    @pl.when(has_prev)
    def _():
        cur_up().start()
        land_up().start()

    @pl.when(has_next)
    def _():
        cur_down().start()
        land_down().start()

    def pack_chunk(c, _):
        bring(c).wait()

        def pack(i, _):
            f = c * chunk + i
            for d in range(nd):
                for w in range(2):
                    own_top[f, w, pl.ds(d, 1), :] = buf[f, d, pl.ds(w, 1), :]
                    own_bot[f, w, pl.ds(d, 1), :] = buf[f, d, pl.ds(nr - 2 + w, 1), :]
            return 0

        lax.fori_loop(0, chunk, pack, 0)

        @pl.when(has_prev)
        def _():
            up(c).start()

        @pl.when(has_next)
        def _():
            down(c).start()

        return 0

    lax.fori_loop(0, chunks, pack_chunk, 0)

    @pl.when(has_prev)
    def _():
        cur_down().wait_recv()
        land_down().wait_recv()

    @pl.when(has_next)
    def _():
        cur_up().wait_recv()
        land_up().wait_recv()

    u, v = load_tiles(cur, 0), load_tiles(cur, 1)
    rt = len(u)
    u_next = next_row(u, load_row(cur_bot, 0, 0))
    u_prev = prev_row(u, load_row(cur_top, 0, SUBS - 1))
    v_next = next_row(v, load_row(cur_bot, 1, 0))
    v_prev = prev_row(v, load_row(cur_top, 1, SUBS - 1))
    store_tiles(ub, [[0.5 * (u[r][c] + u_next[r][c]) for c in range(ct)] for r in range(rt)])
    sea[...] = land[...].astype(F32)
    for r in range(rt):
        u_east, v_east = next_col(u[r]), next_col(v[r])
        u_west, v_west = prev_col(u[r], 0.0), prev_col(v[r], 0.0)
        for c in range(ct):
            at = (pl.ds(r * SUBS, SUBS), pl.ds(c * LANES, LANES))
            vb[at] = 0.5 * (v[r][c] + v_east[c])
            u_dx = 0.5 * (u_next[r][c] - u_prev[r][c])
            v_dx = 0.5 * (v_next[r][c] - v_prev[r][c])
            u_dy = 0.5 * (u_east[c] - u_west[c])
            v_dy = 0.5 * (v_east[c] - v_west[c])
            for d in range(nd + 1):
                k_ref[(d, *at)] = face[0, d] * (u_dx - v_dy) + face[1, d] * u_dy - face[2, d] * v_dx

    def mean(x, y):
        return [0.5 * (p + q) for p, q in zip(x, y)]

    u_rows = [
        load_row(cur_top, 0, SUBS - 2), load_row(cur_top, 0, SUBS - 1), load_row(cur, 0, 0),
        load_row(cur, 0, 1), load_row(cur, 0, nr - 1), load_row(cur_bot, 0, 0), load_row(cur_bot, 0, 1),
    ]
    v_rows = [load_row(cur_top, 1, SUBS - 1), load_row(cur, 1, 0), load_row(cur_bot, 1, 0)]
    kept = [mean(u_rows[i], u_rows[i + 1]) for i in (0, 1, 2, 4, 5)]
    kept += [mean(x, next_col(x)) for x in v_rows]
    kept += [[0.5 * t for t in x] for x in v_rows]
    kept += [
        [t.astype(F32) for t in x]
        for x in (
            load_row(land_top, SUBS - 2), load_row(land_top, SUBS - 1), load_row(land, 0),
            load_row(land, 1), load_row(land, nr - 1), load_row(land_bot, 0), load_row(land_bot, 1),
        )
    ]
    for i, tiles in enumerate(kept):
        for c in range(ct):
            rows[pl.ds(i, 1), pl.ds(c * LANES, LANES)] = tiles[c]

    def edge_step(a, into, out, speed_y, which, land_row):
        v_face, v_half = load_row(rows, 5 + which), load_row(rows, 8 + which)
        east = next_col(a)
        flux = [pick(speed_y[c] + v_face[c], a[c], east[c]) for c in range(ct)]
        west = prev_col(flux, jnp.minimum(speed_y[0] + v_half[0], 0.0) * a[0])
        return [
            land_row[c] * (a[c] - ((out[c] - into[c]) + (flux[c] - west[c]))) for c in range(ct)
        ]

    def edges(f):
        speed_x = [gs[f] * t for t in split_cols(cosb[...])]
        speed_y = [gs[f] * t for t in split_cols(sinb[...])]
        lands = [load_row(rows, 11 + i) for i in range(7)]

        def cells(ref, w, i):
            return [lands[i][c] * t for c, t in enumerate(split_cols(ref[f, w]))]

        def across(i, behind, ahead):
            u_face = load_row(rows, i)
            return [pick(speed_x[c] + u_face[c], behind[c], ahead[c]) for c in range(ct)]

        p2, p1 = cells(halo_top, 0, 0), cells(halo_top, 1, 1)
        a0, a1 = cells(own_top, 0, 2), cells(own_top, 1, 3)
        f_far, f_top, f_in = across(0, p2, p1), across(1, p1, a0), across(2, a0, a1)
        above = edge_step(p1, f_far, f_top, speed_y, 0, lands[1])
        first = edge_step(a0, f_top, f_in, speed_y, 1, lands[2])
        f_top2 = across(1, above, first)
        last = cells(own_bot, 1, 4)
        n0, n1 = cells(halo_bot, 0, 5), cells(halo_bot, 1, 6)
        below = edge_step(n0, across(3, last, n0), across(4, n0, n1), speed_y, 2, lands[5])
        for i, tiles in enumerate((f_top, f_top2, n0, below)):
            for c in range(ct):
                border[i, :, pl.ds(c * LANES, LANES)] = tiles[c]

    def one(f, d):
        speed_x, speed_y = gs[f] * trig[0, d], gs[f] * trig[1, d]
        lands = load_tiles(sea)
        cx = [[speed_x + t for t in row] for row in load_tiles(ub)]
        cy = [[speed_y + t for t in row] for row in load_tiles(vb)]
        out_west = [
            jnp.minimum(speed_y + 0.5 * cur[1, pl.ds(r * SUBS, SUBS), pl.ds(0, LANES)], 0.0)
            for r in range(rt)
        ]
        a = load_tiles(buf, f, d)
        a = [[lands[r][c] * a[r][c] for c in range(ct)] for r in range(rt)]
        for step in range(2):
            south = next_row(a, load_row(border, 2 + step, d))
            fx = [[pick(cx[r][c], a[r][c], south[r][c]) for c in range(ct)] for r in range(rt)]
            fx_prev = prev_row(fx, load_row(border, step, d))
            new = []
            for r in range(rt):
                east = next_col(a[r])
                fy = [pick(cy[r][c], a[r][c], east[c]) for c in range(ct)]
                fy_prev = prev_col(fy, out_west[r] * a[r][0])
                new.append([
                    lands[r][c] * (a[r][c] - ((fx[r][c] - fx_prev[r][c]) + (fy[c] - fy_prev[c])))
                    for c in range(ct)
                ])
            a = new
        store_tiles(buf, a, f, d)

    def work_chunk(c, _):
        @pl.when(has_prev)
        def _():
            down(c).wait_recv()

        @pl.when(has_next)
        def _():
            up(c).wait_recv()

        def work(i, _):
            f = c * chunk + i
            edges(f)

            for d in range(nd):
                one(f, d)
            if sides == 1:
                sel[0, f] = jnp.where(k_ref[0] > 0.0, buf[f, nd - 1], buf[f, 0])
            else:
                sel[0, f] = buf[f, nd - 1]
                sel[1, f] = buf[f, 0]
            return 0

        lax.fori_loop(0, chunk, work, 0)
        put(c).start()
        for side in range(sides):
            turn(side, c).start()
        return 0

    lax.fori_loop(0, chunks, work_chunk, 0)

    def finish(c, _):
        put(c).wait()
        for side in range(sides):
            turn(side, c).wait()

        @pl.when(has_prev)
        def _():
            up(c).wait_send()

        @pl.when(has_next)
        def _():
            down(c).wait_send()

        return 0

    lax.fori_loop(0, chunks, finish, 0)

    @pl.when(has_prev)
    def _():
        cur_up().wait_send()
        land_up().wait_send()

    @pl.when(has_next)
    def _():
        cur_down().wait_send()
        land_down().wait_send()


def refract_kernel(a2, got, k_ref, table, weight, new, stress):
    nf, nd, nr, nc = a2.shape
    step = pl.program_id(0)

    @pl.when(step == 0)
    def _():
        stress[...] = jnp.zeros(stress.shape, F32)

    def work(i, _):
        f = step * nf + i
        for r in range(nr // SUBS):
            for c in range(nc // LANES):
                at = (pl.ds(r * SUBS, SUBS), pl.ds(c * LANES, LANES))
                here = a2[(i, 0, *at)]
                flux = pick(k_ref[(0, *at)], got[(0, i, *at)], here)
                total = even = odd = None
                for d in range(nd):
                    ahead = a2[(i, d + 1, *at)] if d + 1 < nd else got[(got.shape[0] - 1, i, *at)]
                    after = pick(k_ref[(d + 1, *at)], here, ahead)
                    value = here - (after - flux)
                    new[(i, d, *at)] = value
                    p, q = table[0, d] * value, table[1, d] * value
                    total = value if d == 0 else total + value
                    even = p if d == 0 else even + p
                    odd = q if d == 0 else odd + q
                    here, flux = ahead, after
                w, wr = weight[0, f], weight[1, f]
                half = (0.5 * w) * total
                stress[(0, *at)] += wr * (total + even) - half
                stress[(1, *at)] += wr * odd
                stress[(2, *at)] += wr * ((total + total) - even) - half
        return 0

    lax.fori_loop(0, nf, work, 0)


def with_rows(value, axis):
    count, length = lax.axis_size(axis), value.shape[1]
    up = [(i, i + 1) for i in range(count - 1)]
    before = lax.ppermute(value[:, length - 1:], axis, up)
    after = lax.ppermute(value[:, :1], axis, [(j, i) for i, j in up])
    return jnp.concatenate([before, value, after], axis=1)


def col_slope(values):
    padded = jnp.pad(values[1:-1], ((0, 0), (1, 1)))
    return 0.5 * (padded[:, 2:] - padded[:, :-2])


def row_slope(values):
    return 0.5 * (values[2:] - values[:-2])


def per_device(action, currents, land_mask, group_speed, group_ratio, bin_weight):
    nf, nd, nr, nc = action.shape
    n_pts, n_dir = lax.axis_size("pts"), lax.axis_size("dir")
    total_dirs = nd * n_dir
    step_angle = 2.0 * math.pi / total_dirs
    offset = lax.axis_index("dir") * nd
    angles = (offset + jnp.arange(nd)).astype(F32) * step_angle
    trig = jnp.stack([jnp.cos(angles), jnp.sin(angles)])
    face_offset = 0 if n_dir == 2 else offset
    face_index = jnp.arange(nd + 1)
    if n_dir == 2:
        face_index = face_index % nd
    face_angles = ((face_offset + face_index).astype(F32) - 0.5) * step_angle
    scale = total_dirs / (2.0 * math.pi)
    fs, fc = jnp.sin(face_angles), jnp.cos(face_angles)
    face = scale * jnp.stack([fs * fc, fs * fs, fc * fc])
    cosb = jnp.broadcast_to(trig[0][:, None], (nd, nc))
    sinb = jnp.broadcast_to(trig[1][:, None], (nd, nc))
    chunk = max(c for c in range(1, 6) if nf % c == 0)
    chunks = nf // chunk
    sides = 1 if n_dir == 2 else 2
    vmem = pl.BlockSpec(memory_space=pltpu.VMEM)
    smem = pl.BlockSpec(memory_space=pltpu.SMEM)
    hbm = pl.BlockSpec(memory_space=pl.ANY)
    dma = pltpu.SemaphoreType.DMA
    halo = pltpu.VMEM((nf, 2, nd, nc), F32)
    a2, got, turning = pl.pallas_call(
        functools.partial(transport_kernel, n_pts, n_dir, chunk),
        out_shape=(
            jax.ShapeDtypeStruct(action.shape, F32),
            jax.ShapeDtypeStruct((sides, nf, nr, nc), F32),
            jax.ShapeDtypeStruct((nd + 1, nr, nc), F32),
        ),
        in_specs=[hbm, vmem, vmem, smem, smem, vmem, vmem, smem],
        out_specs=(hbm, hbm, vmem),
        scratch_shapes=[
            pltpu.VMEM(action.shape, F32), halo, halo, halo, halo,
            pltpu.VMEM((2, SUBS, nc), F32), pltpu.VMEM((2, SUBS, nc), F32),
            pltpu.VMEM((SUBS, nc), jnp.int32), pltpu.VMEM((SUBS, nc), jnp.int32),
            pltpu.VMEM((nr, nc), F32), pltpu.VMEM((nr, nc), F32), pltpu.VMEM((nr, nc), F32),
            pltpu.VMEM((24, nc), F32), pltpu.VMEM((4, nd, nc), F32),
            pltpu.VMEM((sides, nf, nr, nc), F32),
            dma((chunks,)), dma((chunks,)), dma((chunks,)), dma((chunks,)), dma((chunks,)),
            dma((chunks,)), dma((8,)), dma((sides, chunks)), dma((sides, chunks)),
        ],
        compiler_params=pltpu.CompilerParams(
            collective_id=0, has_side_effects=True, vmem_limit_bytes=40 * 2**20
        ),
        name="transport",
    )(action, currents, land_mask, group_speed, trig, cosb, sinb, face)
    table = jnp.stack([trig[0] * trig[0], trig[0] * trig[1]])
    weight = jnp.stack([bin_weight, bin_weight * group_ratio])
    new_action, stress = pl.pallas_call(
        refract_kernel,
        grid=(chunks,),
        out_shape=(
            jax.ShapeDtypeStruct(action.shape, F32),
            jax.ShapeDtypeStruct((3, nr, nc), F32),
        ),
        in_specs=[
            pl.BlockSpec((chunk, nd, nr, nc), lambda i: (i, 0, 0, 0)),
            pl.BlockSpec((sides, chunk, nr, nc), lambda i: (0, i, 0, 0)),
            pl.BlockSpec((nd + 1, nr, nc), lambda i: (0, 0, 0)),
            smem, smem,
        ],
        out_specs=(
            pl.BlockSpec((chunk, nd, nr, nc), lambda i: (i, 0, 0, 0)),
            pl.BlockSpec((3, nr, nc), lambda i: (0, 0, 0)),
        ),
        compiler_params=pltpu.CompilerParams(vmem_limit_bytes=40 * 2**20),
        name="refract",
    )(a2, got, turning, table, weight)
    ext = lax.psum(with_rows(stress, "pts"), "dir")
    first = -(row_slope(ext[0]) + col_slope(ext[1]))
    second = -(row_slope(ext[1]) + col_slope(ext[2]))
    return new_action, jnp.stack([first, second])


def solution(mesh):
    in_specs = (P(None, "dir", "pts", None), P(None, "pts", None), P("pts", None), P(), P(), P())
    out_specs = (P(None, "dir", "pts", None), P(None, "pts", None))
    return jax.shard_map(
        per_device, mesh=mesh, in_specs=in_specs, out_specs=out_specs, check_vma=False
    )
```

```python
import functools
import math

import jax
import jax.numpy as jnp
import numpy as np
from jax import lax
from jax.experimental import pallas as pl
from jax.experimental.pallas import tpu as pltpu
from jax.sharding import PartitionSpec as P

MESH = pl.DeviceIdType.MESH
LANES = 128
SUBS = 8
F32 = jnp.float32


def lane_of(shape):
    return lax.broadcasted_iota(jnp.int32, shape, 1)


def next_col(tiles):
    count = len(tiles)
    edge = lane_of(tiles[0].shape) == LANES - 1
    rolled = [pltpu.roll(t, LANES - 1, 1) for t in tiles]
    return [
        jnp.where(edge, rolled[c + 1] if c + 1 < count else 0.0, rolled[c])
        for c in range(count)
    ]


def prev_col(tiles, first):
    edge = lane_of(tiles[0].shape) == 0
    rolled = [pltpu.roll(t, 1, 1) for t in tiles]
    return [jnp.where(edge, rolled[c - 1] if c else first, rolled[c]) for c in range(len(tiles))]


def next_row(tiles, below):
    count = len(tiles)
    edge = lax.broadcasted_iota(jnp.int32, (SUBS, LANES), 0) == SUBS - 1
    rolled = [[pltpu.roll(t, SUBS - 1, 0) for t in row] for row in tiles]
    return [
        [
            jnp.where(edge, rolled[r + 1][c] if r + 1 < count else below[c], rolled[r][c])
            for c in range(len(below))
        ]
        for r in range(count)
    ]


def prev_row(tiles, above):
    edge = lax.broadcasted_iota(jnp.int32, (SUBS, LANES), 0) == 0
    rolled = [[pltpu.roll(t, 1, 0) for t in row] for row in tiles]
    return [
        [jnp.where(edge, rolled[r - 1][c] if r else above[c], rolled[r][c]) for c in range(len(above))]
        for r in range(len(tiles))
    ]


def split_cols(value):
    return [value[:, c * LANES:(c + 1) * LANES] for c in range(value.shape[1] // LANES)]


def load_tiles(ref, *lead):
    rows, cols = ref.shape[-2:]
    return [
        [
            ref[(*lead, pl.ds(r * SUBS, SUBS), pl.ds(c * LANES, LANES))]
            for c in range(cols // LANES)
        ]
        for r in range(rows // SUBS)
    ]


def load_row(ref, *lead):
    cols = ref.shape[-1]
    *head, row = lead
    return [ref[(*head, pl.ds(row, 1), pl.ds(c * LANES, LANES))] for c in range(cols // LANES)]


def store_tiles(ref, tiles, *lead):
    for r, row in enumerate(tiles):
        for c, tile in enumerate(row):
            ref[(*lead, pl.ds(r * SUBS, SUBS), pl.ds(c * LANES, LANES))] = tile


def pick(speed, behind, ahead):
    return speed * jnp.where(speed > 0.0, behind, ahead)


def transport_kernel(
    n_pts, n_dir, chunk,
    act, cur, land, gs, weight, table, wave,
    buf, stress,
    got, k_ref, own_top, own_bot, halo_top, halo_bot, cur_top, cur_bot, land_top, land_bot,
    ub, vb, sea, rows, border, sel,
    in_sem, up_send, up_recv, down_send, down_recv, cur_sem, dir_send, dir_recv,
):
    nf, nd, nr, nc = buf.shape
    chunks = nf // chunk
    ct = nc // LANES
    me = lax.axis_index("pts")
    mine = lax.axis_index("dir")
    has_prev = me > 0
    has_next = me < n_pts - 1
    before = jnp.maximum(me - 1, 0)
    after = jnp.minimum(me + 1, n_pts - 1)
    dir_after = lax.rem(mine + 1, n_dir)
    dir_before = lax.rem(mine + n_dir - 1, n_dir)

    def bring(c):
        part = pl.ds(c * chunk, chunk)
        return pltpu.make_async_copy(act.at[part], buf.at[part], in_sem.at[c])

    def remote(src, dst, send, recv, where):
        return pltpu.make_async_remote_copy(
            src_ref=src, dst_ref=dst, send_sem=send, recv_sem=recv,
            device_id=where, device_id_type=MESH,
        )

    def up(c):
        part = pl.ds(c * chunk, chunk)
        return remote(own_top.at[part], halo_bot.at[part], up_send.at[c], up_recv.at[c], {"pts": before})

    def down(c):
        part = pl.ds(c * chunk, chunk)
        return remote(own_bot.at[part], halo_top.at[part], down_send.at[c], down_recv.at[c], {"pts": after})

    def cur_up():
        return remote(cur.at[:, pl.ds(0, SUBS)], cur_bot, cur_sem.at[0], cur_sem.at[1], {"pts": before})

    def cur_down():
        return remote(cur.at[:, pl.ds(nr - SUBS, SUBS)], cur_top, cur_sem.at[2], cur_sem.at[3], {"pts": after})

    def land_up():
        return remote(land.at[pl.ds(0, SUBS)], land_bot, cur_sem.at[4], cur_sem.at[5], {"pts": before})

    def land_down():
        return remote(land.at[pl.ds(nr - SUBS, SUBS)], land_top, cur_sem.at[6], cur_sem.at[7], {"pts": after})

    def turn(side, c):
        part = pl.ds(c * chunk, chunk)
        return remote(
            sel.at[side, part], got.at[side, part], dir_send.at[side, c], dir_recv.at[side, c],
            {"dir": dir_after if side == 0 else dir_before},
        )

    sides = sel.shape[0]

    def start_in(c, _):
        bring(c).start()
        return 0

    lax.fori_loop(0, chunks, start_in, 0)

    barrier = pltpu.get_barrier_semaphore()

    @pl.when(has_prev)
    def _():
        pl.semaphore_signal(barrier, inc=1, device_id={"pts": before}, device_id_type=MESH)

    @pl.when(has_next)
    def _():
        pl.semaphore_signal(barrier, inc=1, device_id={"pts": after}, device_id_type=MESH)

    pl.semaphore_signal(barrier, inc=1, device_id={"dir": dir_after}, device_id_type=MESH)
    if n_dir > 2:
        pl.semaphore_signal(barrier, inc=1, device_id={"dir": dir_before}, device_id_type=MESH)

    @pl.when(jnp.logical_not(has_prev))
    def _():
        def clear(f, _):
            halo_top[f] = jnp.zeros(halo_top.shape[1:], F32)
            return 0
        lax.fori_loop(0, nf, clear, 0)
        cur_top[...] = jnp.zeros(cur_top.shape, F32)
        land_top[...] = jnp.zeros(land_top.shape, jnp.int32)

    @pl.when(jnp.logical_not(has_next))
    def _():
        def clear(f, _):
            halo_bot[f] = jnp.zeros(halo_bot.shape[1:], F32)
            return 0
        lax.fori_loop(0, nf, clear, 0)
        cur_bot[...] = jnp.zeros(cur_bot.shape, F32)
        land_bot[...] = jnp.zeros(land_bot.shape, jnp.int32)

    others = has_prev.astype(jnp.int32) + has_next.astype(jnp.int32)
    pl.semaphore_wait(barrier, others + (2 if n_dir > 2 else 1))

    @pl.when(has_prev)
    def _():
        cur_up().start()
        land_up().start()

    @pl.when(has_next)
    def _():
        cur_down().start()
        land_down().start()

    def pack_chunk(c, _):
        bring(c).wait()

        def pack(i, _):
            f = c * chunk + i
            for d in range(nd):
                for w in range(2):
                    own_top[f, w, pl.ds(d, 1), :] = buf[f, d, pl.ds(w, 1), :]
                    own_bot[f, w, pl.ds(d, 1), :] = buf[f, d, pl.ds(nr - 2 + w, 1), :]
            return 0

        lax.fori_loop(0, chunk, pack, 0)

        @pl.when(has_prev)
        def _():
            up(c).start()

        @pl.when(has_next)
        def _():
            down(c).start()

        return 0

    lax.fori_loop(0, chunks, pack_chunk, 0)

    @pl.when(has_prev)
    def _():
        cur_down().wait_recv()
        land_down().wait_recv()

    @pl.when(has_next)
    def _():
        cur_up().wait_recv()
        land_up().wait_recv()

    u, v = load_tiles(cur, 0), load_tiles(cur, 1)
    rt = len(u)
    u_next = next_row(u, load_row(cur_bot, 0, 0))
    u_prev = prev_row(u, load_row(cur_top, 0, SUBS - 1))
    v_next = next_row(v, load_row(cur_bot, 1, 0))
    v_prev = prev_row(v, load_row(cur_top, 1, SUBS - 1))
    store_tiles(ub, [[0.5 * (u[r][c] + u_next[r][c]) for c in range(ct)] for r in range(rt)])
    sea[...] = land[...].astype(F32)
    for r in range(rt):
        u_east, v_east = next_col(u[r]), next_col(v[r])
        u_west, v_west = prev_col(u[r], 0.0), prev_col(v[r], 0.0)
        for c in range(ct):
            at = (pl.ds(r * SUBS, SUBS), pl.ds(c * LANES, LANES))
            vb[at] = 0.5 * (v[r][c] + v_east[c])
            u_dx = 0.5 * (u_next[r][c] - u_prev[r][c])
            v_dx = 0.5 * (v_next[r][c] - v_prev[r][c])
            u_dy = 0.5 * (u_east[c] - u_west[c])
            v_dy = 0.5 * (v_east[c] - v_west[c])
            for d in range(nd + 1):
                k_ref[(d, *at)] = table[mine, 2, d] * (u_dx - v_dy) + table[mine, 3, d] * u_dy - table[mine, 4, d] * v_dx

    def mean(x, y):
        return [0.5 * (p + q) for p, q in zip(x, y)]

    u_rows = [
        load_row(cur_top, 0, SUBS - 2), load_row(cur_top, 0, SUBS - 1), load_row(cur, 0, 0),
        load_row(cur, 0, 1), load_row(cur, 0, nr - 1), load_row(cur_bot, 0, 0), load_row(cur_bot, 0, 1),
    ]
    v_rows = [load_row(cur_top, 1, SUBS - 1), load_row(cur, 1, 0), load_row(cur_bot, 1, 0)]
    kept = [mean(u_rows[i], u_rows[i + 1]) for i in (0, 1, 2, 4, 5)]
    kept += [mean(x, next_col(x)) for x in v_rows]
    kept += [[0.5 * t for t in x] for x in v_rows]
    kept += [
        [t.astype(F32) for t in x]
        for x in (
            load_row(land_top, SUBS - 2), load_row(land_top, SUBS - 1), load_row(land, 0),
            load_row(land, 1), load_row(land, nr - 1), load_row(land_bot, 0), load_row(land_bot, 1),
        )
    ]
    for i, tiles in enumerate(kept):
        for c in range(ct):
            rows[pl.ds(i, 1), pl.ds(c * LANES, LANES)] = tiles[c]

    def edge_step(a, into, out, speed_y, which, land_row):
        v_face, v_half = load_row(rows, 5 + which), load_row(rows, 8 + which)
        east = next_col(a)
        flux = [pick(speed_y[c] + v_face[c], a[c], east[c]) for c in range(ct)]
        west = prev_col(flux, jnp.minimum(speed_y[0] + v_half[0], 0.0) * a[0])
        return [
            land_row[c] * (a[c] - ((out[c] - into[c]) + (flux[c] - west[c]))) for c in range(ct)
        ]

    def edges(f):
        speed_x = [gs[f] * t for t in split_cols(wave[mine, 0])]
        speed_y = [gs[f] * t for t in split_cols(wave[mine, 1])]
        lands = [load_row(rows, 11 + i) for i in range(7)]

        def cells(ref, w, i):
            return [lands[i][c] * t for c, t in enumerate(split_cols(ref[f, w]))]

        def across(i, behind, ahead):
            u_face = load_row(rows, i)
            return [pick(speed_x[c] + u_face[c], behind[c], ahead[c]) for c in range(ct)]

        p2, p1 = cells(halo_top, 0, 0), cells(halo_top, 1, 1)
        a0, a1 = cells(own_top, 0, 2), cells(own_top, 1, 3)
        f_far, f_top, f_in = across(0, p2, p1), across(1, p1, a0), across(2, a0, a1)
        above = edge_step(p1, f_far, f_top, speed_y, 0, lands[1])
        first = edge_step(a0, f_top, f_in, speed_y, 1, lands[2])
        f_top2 = across(1, above, first)
        last = cells(own_bot, 1, 4)
        n0, n1 = cells(halo_bot, 0, 5), cells(halo_bot, 1, 6)
        below = edge_step(n0, across(3, last, n0), across(4, n0, n1), speed_y, 2, lands[5])
        for i, tiles in enumerate((f_top, f_top2, n0, below)):
            for c in range(ct):
                border[i, :, pl.ds(c * LANES, LANES)] = tiles[c]

    def one(f, d):
        speed_x, speed_y = gs[f] * table[mine, 0, d], gs[f] * table[mine, 1, d]
        lands = load_tiles(sea)
        cx = [[speed_x + t for t in row] for row in load_tiles(ub)]
        cy = [[speed_y + t for t in row] for row in load_tiles(vb)]
        out_west = [
            jnp.minimum(speed_y + 0.5 * cur[1, pl.ds(r * SUBS, SUBS), pl.ds(0, LANES)], 0.0)
            for r in range(rt)
        ]
        a = load_tiles(buf, f, d)
        a = [[lands[r][c] * a[r][c] for c in range(ct)] for r in range(rt)]
        for step in range(2):
            south = next_row(a, load_row(border, 2 + step, d))
            fx = [[pick(cx[r][c], a[r][c], south[r][c]) for c in range(ct)] for r in range(rt)]
            fx_prev = prev_row(fx, load_row(border, step, d))
            new = []
            for r in range(rt):
                east = next_col(a[r])
                fy = [pick(cy[r][c], a[r][c], east[c]) for c in range(ct)]
                fy_prev = prev_col(fy, out_west[r] * a[r][0])
                new.append([
                    lands[r][c] * (a[r][c] - ((fx[r][c] - fx_prev[r][c]) + (fy[c] - fy_prev[c])))
                    for c in range(ct)
                ])
            a = new
        store_tiles(buf, a, f, d)

    def work_chunk(c, _):
        @pl.when(has_prev)
        def _():
            down(c).wait_recv()

        @pl.when(has_next)
        def _():
            up(c).wait_recv()

        def work(i, _):
            f = c * chunk + i
            edges(f)

            for d in range(nd):
                one(f, d)
            if sides == 1:
                sel[0, f] = jnp.where(k_ref[0] > 0.0, buf[f, nd - 1], buf[f, 0])
            else:
                sel[0, f] = buf[f, nd - 1]
                sel[1, f] = buf[f, 0]
            return 0

        lax.fori_loop(0, chunk, work, 0)
        for side in range(sides):
            turn(side, c).start()

        @pl.when(c > 0)
        def _():
            refract_chunk(c - 1)

        return 0

    def refract_chunk(c):
        for side in range(sides):
            turn(side, c).wait_recv()

        def work(i, _):
            refract(c * chunk + i)
            return 0

        lax.fori_loop(0, chunk, work, 0)

    def refract(f):
        for r in range(rt):
            for q in range(ct):
                at = (pl.ds(r * SUBS, SUBS), pl.ds(q * LANES, LANES))
                here = buf[(f, 0, *at)]
                flux = pick(k_ref[(0, *at)], got[(0, f, *at)], here)
                total = even = odd = None
                for d in range(nd):
                    ahead = buf[(f, d + 1, *at)] if d + 1 < nd else got[(sides - 1, f, *at)]
                    after_d = pick(k_ref[(d + 1, *at)], here, ahead)
                    value = here - (after_d - flux)
                    buf[(f, d, *at)] = value
                    x, y = table[mine, 5, d] * value, table[mine, 6, d] * value
                    total = value if d == 0 else total + value
                    even = x if d == 0 else even + x
                    odd = y if d == 0 else odd + y
                    here, flux = ahead, after_d
                w, wr = weight[0, f], weight[1, f]
                half = (0.5 * w) * total
                stress[(0, *at)] += wr * (total + even) - half
                stress[(1, *at)] += wr * odd
                stress[(2, *at)] += wr * ((total + total) - even) - half

    stress[...] = jnp.zeros(stress.shape, F32)
    lax.fori_loop(0, chunks, work_chunk, 0)
    refract_chunk(chunks - 1)

    def finish(c, _):
        for side in range(sides):
            turn(side, c).wait_send()

        @pl.when(has_prev)
        def _():
            up(c).wait_send()

        @pl.when(has_next)
        def _():
            down(c).wait_send()

        return 0

    lax.fori_loop(0, chunks, finish, 0)

    @pl.when(has_prev)
    def _():
        cur_up().wait_send()
        land_up().wait_send()

    @pl.when(has_next)
    def _():
        cur_down().wait_send()
        land_down().wait_send()


def force_kernel(n_pts, n_dir, stress, force, full, top, bot, send, recv):
    nr = stress.shape[1]
    me = lax.axis_index("pts")
    mine = lax.axis_index("dir")
    has_prev = me > 0
    has_next = me < n_pts - 1
    before = jnp.maximum(me - 1, 0)
    after = jnp.minimum(me + 1, n_pts - 1)
    barrier = pltpu.get_barrier_semaphore()
    sectors = [lax.rem(mine + j, n_dir) for j in range(n_dir)]

    def greet(point, sector):
        pl.semaphore_signal(
            barrier, inc=1, device_id={"pts": point, "dir": sector}, device_id_type=MESH
        )

    for sector in sectors[1:]:
        greet(me, sector)

    @pl.when(has_prev)
    def _():
        for sector in sectors:
            greet(before, sector)

    @pl.when(has_next)
    def _():
        for sector in sectors:
            greet(after, sector)

    @pl.when(jnp.logical_not(has_prev))
    def _():
        top[...] = jnp.zeros(top.shape, F32)

    @pl.when(jnp.logical_not(has_next))
    def _():
        bot[...] = jnp.zeros(bot.shape, F32)

    full[mine] = stress[...]
    others = has_prev.astype(jnp.int32) + has_next.astype(jnp.int32)
    pl.semaphore_wait(barrier, n_dir * others + n_dir - 1)

    def copy(kind, j, slot):
        src = (
            stress, stress.at[:, pl.ds(nr - SUBS, SUBS)], stress.at[:, pl.ds(0, SUBS)]
        )[kind]
        dst = (full, top, bot)[kind].at[slot]
        return pltpu.make_async_remote_copy(
            src_ref=src, dst_ref=dst, send_sem=send.at[kind, j], recv_sem=recv.at[kind, slot],
            device_id={"pts": (me, after, before)[kind], "dir": sectors[j]}, device_id_type=MESH,
        )

    @pl.when(has_next)
    def _():
        for j in range(n_dir):
            copy(1, j, mine).start()

    @pl.when(has_prev)
    def _():
        for j in range(n_dir):
            copy(2, j, mine).start()

    for j in range(1, n_dir):
        copy(0, j, mine).start()
    for j in range(1, n_dir):
        copy(0, j, sectors[j]).wait_recv()

    @pl.when(has_prev)
    def _():
        for j in range(n_dir):
            copy(1, j, sectors[j]).wait_recv()

    @pl.when(has_next)
    def _():
        for j in range(n_dir):
            copy(2, j, sectors[j]).wait_recv()

    def added(load):
        parts = [load(s) for s in range(n_dir)]
        total = parts[0]
        for part in parts[1:]:
            total = jax.tree.map(jnp.add, total, part)
        return total

    whole = [added(lambda s: load_tiles(full, s, q)) for q in range(3)]
    above = [added(lambda s: load_row(top, s, q, SUBS - 1)) for q in range(3)]
    below = [added(lambda s: load_row(bot, s, q, 0)) for q in range(3)]
    for out in range(2):
        ahead, behind = next_row(whole[out], below[out]), prev_row(whole[out], above[out])
        for r, row in enumerate(whole[out + 1]):
            east, west = next_col(row), prev_col(row, 0.0)
            for c in range(len(row)):
                force[out, pl.ds(r * SUBS, SUBS), pl.ds(c * LANES, LANES)] = -(
                    0.5 * (ahead[r][c] - behind[r][c]) + 0.5 * (east[c] - west[c])
                )

    for j in range(1, n_dir):
        copy(0, j, mine).wait_send()

    @pl.when(has_next)
    def _():
        for j in range(n_dir):
            copy(1, j, mine).wait_send()

    @pl.when(has_prev)
    def _():
        for j in range(n_dir):
            copy(2, j, mine).wait_send()


def geometry(n_dir, nd):
    total = n_dir * nd
    step = 2.0 * math.pi / total
    out = np.zeros((n_dir, 7, nd + 1), np.float32)
    for s in range(n_dir):
        angle = (s * nd + np.arange(nd)) * step
        index = np.arange(nd + 1) % nd if n_dir == 2 else s * nd + np.arange(nd + 1)
        phi = (index - 0.5) * step
        scale = total / (2.0 * math.pi)
        cos, sin = np.cos(angle), np.sin(angle)
        out[s, 0, :nd], out[s, 1, :nd] = cos, sin
        out[s, 2] = scale * np.sin(phi) * np.cos(phi)
        out[s, 3] = scale * np.sin(phi) ** 2
        out[s, 4] = scale * np.cos(phi) ** 2
        out[s, 5, :nd], out[s, 6, :nd] = cos * cos, sin * cos
    return out


def per_device(action, currents, land_mask, group_speed, group_ratio, bin_weight):
    nf, nd, nr, nc = action.shape
    n_pts, n_dir = lax.axis_size("pts"), lax.axis_size("dir")
    table = geometry(n_dir, nd)
    wave = np.ascontiguousarray(np.broadcast_to(table[:, :2, :nd, None], (n_dir, 2, nd, nc)))
    chunk = max(c for c in range(1, 6) if nf % c == 0)
    chunks = nf // chunk
    sides = 1 if n_dir == 2 else 2
    vmem = pl.BlockSpec(memory_space=pltpu.VMEM)
    smem = pl.BlockSpec(memory_space=pltpu.SMEM)
    hbm = pl.BlockSpec(memory_space=pl.ANY)
    dma = pltpu.SemaphoreType.DMA
    halo = pltpu.VMEM((nf, 2, nd, nc), F32)
    weight = jnp.stack([bin_weight, bin_weight * group_ratio])
    new_action, stress = pl.pallas_call(
        functools.partial(transport_kernel, n_pts, n_dir, chunk),
        out_shape=(
            jax.ShapeDtypeStruct(action.shape, F32),
            jax.ShapeDtypeStruct((3, nr, nc), F32),
        ),
        in_specs=[hbm, vmem, vmem, smem, smem, smem, vmem],
        out_specs=(vmem, vmem),
        scratch_shapes=[
            pltpu.VMEM((sides, nf, nr, nc), F32), pltpu.VMEM((nd + 1, nr, nc), F32),
            halo, halo, halo, halo,
            pltpu.VMEM((2, SUBS, nc), F32), pltpu.VMEM((2, SUBS, nc), F32),
            pltpu.VMEM((SUBS, nc), jnp.int32), pltpu.VMEM((SUBS, nc), jnp.int32),
            pltpu.VMEM((nr, nc), F32), pltpu.VMEM((nr, nc), F32), pltpu.VMEM((nr, nc), F32),
            pltpu.VMEM((24, nc), F32), pltpu.VMEM((4, nd, nc), F32),
            pltpu.VMEM((sides, nf, nr, nc), F32),
            dma((chunks,)), dma((chunks,)), dma((chunks,)), dma((chunks,)),
            dma((chunks,)), dma((8,)), dma((sides, chunks)), dma((sides, chunks)),
        ],
        compiler_params=pltpu.CompilerParams(
            collective_id=0, has_side_effects=True, vmem_limit_bytes=32 * 2**20
        ),
        name="transport",
    )(action, currents, land_mask, group_speed, weight, table, wave)
    force = pl.pallas_call(
        functools.partial(force_kernel, n_pts, n_dir),
        out_shape=jax.ShapeDtypeStruct((2, nr, nc), F32),
        in_specs=[vmem],
        out_specs=vmem,
        scratch_shapes=[
            pltpu.VMEM((n_dir, 3, nr, nc), F32),
            pltpu.VMEM((n_dir, 3, SUBS, nc), F32), pltpu.VMEM((n_dir, 3, SUBS, nc), F32),
            dma((3, n_dir)), dma((3, n_dir)),
        ],
        compiler_params=pltpu.CompilerParams(
            collective_id=1, has_side_effects=True, vmem_limit_bytes=16 * 2**20
        ),
        cost_estimate=pl.CostEstimate(flops=10**6, bytes_accessed=2 * 10**7, transcendentals=0),
        name="force",
    )(stress)
    return new_action, force


def solution(mesh):
    in_specs = (P(None, "dir", "pts", None), P(None, "pts", None), P("pts", None), P(), P(), P())
    out_specs = (P(None, "dir", "pts", None), P(None, "pts", None))
    return jax.shard_map(
        per_device, mesh=mesh, in_specs=in_specs, out_specs=out_specs, check_vma=False
    )
```

```python
import functools
import math

import jax
import jax.numpy as jnp
import numpy as np
from jax import lax
from jax.experimental import pallas as pl
from jax.experimental.pallas import tpu as pltpu
from jax.sharding import PartitionSpec as P

MESH = pl.DeviceIdType.MESH
LANES = 128
SUBS = 8
F32 = jnp.float32


def lane_of(shape):
    return lax.broadcasted_iota(jnp.int32, shape, 1)


def next_col(tiles):
    count = len(tiles)
    edge = lane_of(tiles[0].shape) == LANES - 1
    rolled = [pltpu.roll(t, LANES - 1, 1) for t in tiles]
    return [
        jnp.where(edge, rolled[c + 1] if c + 1 < count else 0.0, rolled[c])
        for c in range(count)
    ]


def prev_col(tiles, first):
    edge = lane_of(tiles[0].shape) == 0
    rolled = [pltpu.roll(t, 1, 1) for t in tiles]
    return [jnp.where(edge, rolled[c - 1] if c else first, rolled[c]) for c in range(len(tiles))]


def next_row(tiles, below):
    count = len(tiles)
    edge = lax.broadcasted_iota(jnp.int32, (SUBS, LANES), 0) == SUBS - 1
    rolled = [[pltpu.roll(t, SUBS - 1, 0) for t in row] for row in tiles]
    return [
        [
            jnp.where(edge, rolled[r + 1][c] if r + 1 < count else below[c], rolled[r][c])
            for c in range(len(below))
        ]
        for r in range(count)
    ]


def prev_row(tiles, above):
    edge = lax.broadcasted_iota(jnp.int32, (SUBS, LANES), 0) == 0
    rolled = [[pltpu.roll(t, 1, 0) for t in row] for row in tiles]
    return [
        [jnp.where(edge, rolled[r - 1][c] if r else above[c], rolled[r][c]) for c in range(len(above))]
        for r in range(len(tiles))
    ]


def split_cols(value):
    return [value[:, c * LANES:(c + 1) * LANES] for c in range(value.shape[1] // LANES)]


def load_tiles(ref, *lead):
    rows, cols = ref.shape[-2:]
    return [
        [
            ref[(*lead, pl.ds(r * SUBS, SUBS), pl.ds(c * LANES, LANES))]
            for c in range(cols // LANES)
        ]
        for r in range(rows // SUBS)
    ]


def load_row(ref, *lead):
    cols = ref.shape[-1]
    *head, row = lead
    return [ref[(*head, pl.ds(row, 1), pl.ds(c * LANES, LANES))] for c in range(cols // LANES)]


def store_tiles(ref, tiles, *lead):
    for r, row in enumerate(tiles):
        for c, tile in enumerate(row):
            ref[(*lead, pl.ds(r * SUBS, SUBS), pl.ds(c * LANES, LANES))] = tile


def pick(speed, behind, ahead):
    return speed * jnp.where(speed > 0.0, behind, ahead)


def transport_kernel(
    n_pts, n_dir, chunk,
    act, cur_in, land_in, wave_in, gs, table,
    a2, got, k_out,
    buf, cur, land, wave, k_ref, own_top, own_bot, halo_top, halo_bot, cur_top, cur_bot, land_top, land_bot,
    ub, vb, sea, rows, border, sel,
    in_sem, out_sem, small_sem, up_send, up_recv, down_send, down_recv, cur_sem, dir_send, dir_recv,
):
    nf, nd, nr, nc = buf.shape
    chunks = nf // chunk
    ct = nc // LANES
    me = lax.axis_index("pts")
    mine = lax.axis_index("dir")
    has_prev = me > 0
    has_next = me < n_pts - 1
    before = jnp.maximum(me - 1, 0)
    after = jnp.minimum(me + 1, n_pts - 1)
    dir_after = lax.rem(mine + 1, n_dir)
    dir_before = lax.rem(mine + n_dir - 1, n_dir)

    def bring(c):
        part = pl.ds(c * chunk, chunk)
        return pltpu.make_async_copy(act.at[part], buf.at[part], in_sem.at[c])

    def put(c):
        part = pl.ds(c * chunk, chunk)
        return pltpu.make_async_copy(buf.at[part], a2.at[part], out_sem.at[c])

    small = [
        pltpu.make_async_copy(src, dst, small_sem.at[i])
        for i, (src, dst) in enumerate(((cur_in, cur), (land_in, land), (wave_in, wave)))
    ]
    put_turning = pltpu.make_async_copy(k_ref, k_out, small_sem.at[3])

    def remote(src, dst, send, recv, where):
        return pltpu.make_async_remote_copy(
            src_ref=src, dst_ref=dst, send_sem=send, recv_sem=recv,
            device_id=where, device_id_type=MESH,
        )

    def up(c):
        part = pl.ds(c * chunk, chunk)
        return remote(own_top.at[part], halo_bot.at[part], up_send.at[c], up_recv.at[c], {"pts": before})

    def down(c):
        part = pl.ds(c * chunk, chunk)
        return remote(own_bot.at[part], halo_top.at[part], down_send.at[c], down_recv.at[c], {"pts": after})

    def cur_up():
        return remote(cur.at[:, pl.ds(0, SUBS)], cur_bot, cur_sem.at[0], cur_sem.at[1], {"pts": before})

    def cur_down():
        return remote(cur.at[:, pl.ds(nr - SUBS, SUBS)], cur_top, cur_sem.at[2], cur_sem.at[3], {"pts": after})

    def land_up():
        return remote(land.at[pl.ds(0, SUBS)], land_bot, cur_sem.at[4], cur_sem.at[5], {"pts": before})

    def land_down():
        return remote(land.at[pl.ds(nr - SUBS, SUBS)], land_top, cur_sem.at[6], cur_sem.at[7], {"pts": after})

    def turn(side, c):
        part = pl.ds(c * chunk, chunk)
        return remote(
            sel.at[side, part], got.at[side, part], dir_send.at[side, c], dir_recv.at[side, c],
            {"dir": dir_after if side == 0 else dir_before},
        )

    sides = sel.shape[0]

    for one_copy in small:
        one_copy.start()

    def start_in(c, _):
        bring(c).start()
        return 0

    lax.fori_loop(0, chunks, start_in, 0)

    barrier = pltpu.get_barrier_semaphore()

    @pl.when(has_prev)
    def _():
        pl.semaphore_signal(barrier, inc=1, device_id={"pts": before}, device_id_type=MESH)

    @pl.when(has_next)
    def _():
        pl.semaphore_signal(barrier, inc=1, device_id={"pts": after}, device_id_type=MESH)

    pl.semaphore_signal(barrier, inc=1, device_id={"dir": dir_after}, device_id_type=MESH)
    if n_dir > 2:
        pl.semaphore_signal(barrier, inc=1, device_id={"dir": dir_before}, device_id_type=MESH)

    @pl.when(jnp.logical_not(has_prev))
    def _():
        def clear(f, _):
            halo_top[f] = jnp.zeros(halo_top.shape[1:], F32)
            return 0
        lax.fori_loop(0, nf, clear, 0)
        cur_top[...] = jnp.zeros(cur_top.shape, F32)
        land_top[...] = jnp.zeros(land_top.shape, jnp.int32)

    @pl.when(jnp.logical_not(has_next))
    def _():
        def clear(f, _):
            halo_bot[f] = jnp.zeros(halo_bot.shape[1:], F32)
            return 0
        lax.fori_loop(0, nf, clear, 0)
        cur_bot[...] = jnp.zeros(cur_bot.shape, F32)
        land_bot[...] = jnp.zeros(land_bot.shape, jnp.int32)

    others = has_prev.astype(jnp.int32) + has_next.astype(jnp.int32)
    pl.semaphore_wait(barrier, others + (2 if n_dir > 2 else 1))

    for one_copy in small:
        one_copy.wait()

    @pl.when(has_prev)
    def _():
        cur_up().start()
        land_up().start()

    @pl.when(has_next)
    def _():
        cur_down().start()
        land_down().start()

    def pack_chunk(c, _):
        bring(c).wait()

        def pack(i, _):
            f = c * chunk + i
            for d in range(nd):
                for w in range(2):
                    own_top[f, w, pl.ds(d, 1), :] = buf[f, d, pl.ds(w, 1), :]
                    own_bot[f, w, pl.ds(d, 1), :] = buf[f, d, pl.ds(nr - 2 + w, 1), :]
            return 0

        lax.fori_loop(0, chunk, pack, 0)

        @pl.when(has_prev)
        def _():
            up(c).start()

        @pl.when(has_next)
        def _():
            down(c).start()

        return 0

    lax.fori_loop(0, chunks, pack_chunk, 0)

    @pl.when(has_prev)
    def _():
        cur_down().wait_recv()
        land_down().wait_recv()

    @pl.when(has_next)
    def _():
        cur_up().wait_recv()
        land_up().wait_recv()

    u, v = load_tiles(cur, 0), load_tiles(cur, 1)
    rt = len(u)
    u_next = next_row(u, load_row(cur_bot, 0, 0))
    u_prev = prev_row(u, load_row(cur_top, 0, SUBS - 1))
    v_next = next_row(v, load_row(cur_bot, 1, 0))
    v_prev = prev_row(v, load_row(cur_top, 1, SUBS - 1))
    store_tiles(ub, [[0.5 * (u[r][c] + u_next[r][c]) for c in range(ct)] for r in range(rt)])
    sea[...] = land[...].astype(F32)
    for r in range(rt):
        u_east, v_east = next_col(u[r]), next_col(v[r])
        u_west, v_west = prev_col(u[r], 0.0), prev_col(v[r], 0.0)
        for c in range(ct):
            at = (pl.ds(r * SUBS, SUBS), pl.ds(c * LANES, LANES))
            vb[at] = 0.5 * (v[r][c] + v_east[c])
            u_dx = 0.5 * (u_next[r][c] - u_prev[r][c])
            v_dx = 0.5 * (v_next[r][c] - v_prev[r][c])
            u_dy = 0.5 * (u_east[c] - u_west[c])
            v_dy = 0.5 * (v_east[c] - v_west[c])
            for d in range(nd + 1):
                k_ref[(d, *at)] = table[mine, 2, d] * (u_dx - v_dy) + table[mine, 3, d] * u_dy - table[mine, 4, d] * v_dx

    def mean(x, y):
        return [0.5 * (p + q) for p, q in zip(x, y)]

    u_rows = [
        load_row(cur_top, 0, SUBS - 2), load_row(cur_top, 0, SUBS - 1), load_row(cur, 0, 0),
        load_row(cur, 0, 1), load_row(cur, 0, nr - 1), load_row(cur_bot, 0, 0), load_row(cur_bot, 0, 1),
    ]
    v_rows = [load_row(cur_top, 1, SUBS - 1), load_row(cur, 1, 0), load_row(cur_bot, 1, 0)]
    kept = [mean(u_rows[i], u_rows[i + 1]) for i in (0, 1, 2, 4, 5)]
    kept += [mean(x, next_col(x)) for x in v_rows]
    kept += [[0.5 * t for t in x] for x in v_rows]
    kept += [
        [t.astype(F32) for t in x]
        for x in (
            load_row(land_top, SUBS - 2), load_row(land_top, SUBS - 1), load_row(land, 0),
            load_row(land, 1), load_row(land, nr - 1), load_row(land_bot, 0), load_row(land_bot, 1),
        )
    ]
    for i, tiles in enumerate(kept):
        for c in range(ct):
            rows[pl.ds(i, 1), pl.ds(c * LANES, LANES)] = tiles[c]

    def edge_step(a, into, out, speed_y, which, land_row):
        v_face, v_half = load_row(rows, 5 + which), load_row(rows, 8 + which)
        east = next_col(a)
        flux = [pick(speed_y[c] + v_face[c], a[c], east[c]) for c in range(ct)]
        west = prev_col(flux, jnp.minimum(speed_y[0] + v_half[0], 0.0) * a[0])
        return [
            land_row[c] * (a[c] - ((out[c] - into[c]) + (flux[c] - west[c]))) for c in range(ct)
        ]

    def edges(f):
        speed_x = [gs[f] * t for t in split_cols(wave[mine, 0])]
        speed_y = [gs[f] * t for t in split_cols(wave[mine, 1])]
        lands = [load_row(rows, 11 + i) for i in range(7)]

        def cells(ref, w, i):
            return [lands[i][c] * t for c, t in enumerate(split_cols(ref[f, w]))]

        def across(i, behind, ahead):
            u_face = load_row(rows, i)
            return [pick(speed_x[c] + u_face[c], behind[c], ahead[c]) for c in range(ct)]

        p2, p1 = cells(halo_top, 0, 0), cells(halo_top, 1, 1)
        a0, a1 = cells(own_top, 0, 2), cells(own_top, 1, 3)
        f_far, f_top, f_in = across(0, p2, p1), across(1, p1, a0), across(2, a0, a1)
        above = edge_step(p1, f_far, f_top, speed_y, 0, lands[1])
        first = edge_step(a0, f_top, f_in, speed_y, 1, lands[2])
        f_top2 = across(1, above, first)
        last = cells(own_bot, 1, 4)
        n0, n1 = cells(halo_bot, 0, 5), cells(halo_bot, 1, 6)
        below = edge_step(n0, across(3, last, n0), across(4, n0, n1), speed_y, 2, lands[5])
        for i, tiles in enumerate((f_top, f_top2, n0, below)):
            for c in range(ct):
                border[i, :, pl.ds(c * LANES, LANES)] = tiles[c]

    def one(f, d):
        speed_x, speed_y = gs[f] * table[mine, 0, d], gs[f] * table[mine, 1, d]
        lands = load_tiles(sea)
        cx = [[speed_x + t for t in row] for row in load_tiles(ub)]
        cy = [[speed_y + t for t in row] for row in load_tiles(vb)]
        out_west = [
            jnp.minimum(speed_y + 0.5 * cur[1, pl.ds(r * SUBS, SUBS), pl.ds(0, LANES)], 0.0)
            for r in range(rt)
        ]
        a = load_tiles(buf, f, d)
        a = [[lands[r][c] * a[r][c] for c in range(ct)] for r in range(rt)]
        for step in range(2):
            south = next_row(a, load_row(border, 2 + step, d))
            fx = [[pick(cx[r][c], a[r][c], south[r][c]) for c in range(ct)] for r in range(rt)]
            fx_prev = prev_row(fx, load_row(border, step, d))
            new = []
            for r in range(rt):
                east = next_col(a[r])
                fy = [pick(cy[r][c], a[r][c], east[c]) for c in range(ct)]
                fy_prev = prev_col(fy, out_west[r] * a[r][0])
                new.append([
                    lands[r][c] * (a[r][c] - ((fx[r][c] - fx_prev[r][c]) + (fy[c] - fy_prev[c])))
                    for c in range(ct)
                ])
            a = new
        store_tiles(buf, a, f, d)

    def work_chunk(c, _):
        @pl.when(has_prev)
        def _():
            down(c).wait_recv()

        @pl.when(has_next)
        def _():
            up(c).wait_recv()

        def work(i, _):
            f = c * chunk + i
            edges(f)

            for d in range(nd):
                one(f, d)
            if sides == 1:
                sel[0, f] = jnp.where(k_ref[0] > 0.0, buf[f, nd - 1], buf[f, 0])
            else:
                sel[0, f] = buf[f, nd - 1]
                sel[1, f] = buf[f, 0]
            return 0

        lax.fori_loop(0, chunk, work, 0)
        for side in range(sides):
            turn(side, c).start()

        put(c).start()
        return 0

    put_turning.start()
    lax.fori_loop(0, chunks, work_chunk, 0)
    put_turning.wait()

    def finish(c, _):
        for side in range(sides):
            turn(side, c).wait()
        put(c).wait()

        @pl.when(has_prev)
        def _():
            up(c).wait_send()

        @pl.when(has_next)
        def _():
            down(c).wait_send()

        return 0

    lax.fori_loop(0, chunks, finish, 0)

    @pl.when(has_prev)
    def _():
        cur_up().wait_send()
        land_up().wait_send()

    @pl.when(has_next)
    def _():
        cur_down().wait_send()
        land_down().wait_send()


def refract_kernel(a2, got, k_ref, table, wt, ratio, new, stress):
    nf, nd, nr, nc = a2.shape
    step = pl.program_id(0)
    mine = lax.axis_index("dir")

    @pl.when(step == 0)
    def _():
        stress[...] = jnp.zeros(stress.shape, F32)

    def work(i, _):
        f = step * nf + i
        for r in range(nr // SUBS):
            for c in range(nc // LANES):
                at = (pl.ds(r * SUBS, SUBS), pl.ds(c * LANES, LANES))
                here = a2[(i, 0, *at)]
                flux = pick(k_ref[(0, *at)], got[(0, i, *at)], here)
                total = even = odd = None
                for d in range(nd):
                    ahead = a2[(i, d + 1, *at)] if d + 1 < nd else got[(got.shape[0] - 1, i, *at)]
                    after = pick(k_ref[(d + 1, *at)], here, ahead)
                    value = here - (after - flux)
                    new[(i, d, *at)] = value
                    p, q = table[mine, 5, d] * value, table[mine, 6, d] * value
                    total = value if d == 0 else total + value
                    even = p if d == 0 else even + p
                    odd = q if d == 0 else odd + q
                    here, flux = ahead, after
                w = wt[f]
                wr = w * ratio[f]
                half = (0.5 * w) * total
                stress[(0, *at)] += wr * (total + even) - half
                stress[(1, *at)] += wr * odd
                stress[(2, *at)] += wr * ((total + total) - even) - half
        return 0

    lax.fori_loop(0, nf, work, 0)


def force_kernel(n_pts, n_dir, stress, force, full, top, bot, send, recv):
    nr = stress.shape[1]
    me = lax.axis_index("pts")
    mine = lax.axis_index("dir")
    has_prev = me > 0
    has_next = me < n_pts - 1
    before = jnp.maximum(me - 1, 0)
    after = jnp.minimum(me + 1, n_pts - 1)
    barrier = pltpu.get_barrier_semaphore()
    sectors = [lax.rem(mine + j, n_dir) for j in range(n_dir)]

    def greet(point, sector):
        pl.semaphore_signal(
            barrier, inc=1, device_id={"pts": point, "dir": sector}, device_id_type=MESH
        )

    for sector in sectors[1:]:
        greet(me, sector)

    @pl.when(has_prev)
    def _():
        for sector in sectors:
            greet(before, sector)

    @pl.when(has_next)
    def _():
        for sector in sectors:
            greet(after, sector)

    @pl.when(jnp.logical_not(has_prev))
    def _():
        top[...] = jnp.zeros(top.shape, F32)

    @pl.when(jnp.logical_not(has_next))
    def _():
        bot[...] = jnp.zeros(bot.shape, F32)

    full[mine] = stress[...]
    others = has_prev.astype(jnp.int32) + has_next.astype(jnp.int32)
    pl.semaphore_wait(barrier, n_dir * others + n_dir - 1)

    def copy(kind, j, slot):
        src = (
            stress, stress.at[:, pl.ds(nr - SUBS, SUBS)], stress.at[:, pl.ds(0, SUBS)]
        )[kind]
        dst = (full, top, bot)[kind].at[slot]
        return pltpu.make_async_remote_copy(
            src_ref=src, dst_ref=dst, send_sem=send.at[kind, j], recv_sem=recv.at[kind, slot],
            device_id={"pts": (me, after, before)[kind], "dir": sectors[j]}, device_id_type=MESH,
        )

    @pl.when(has_next)
    def _():
        for j in range(n_dir):
            copy(1, j, mine).start()

    @pl.when(has_prev)
    def _():
        for j in range(n_dir):
            copy(2, j, mine).start()

    for j in range(1, n_dir):
        copy(0, j, mine).start()
    for j in range(1, n_dir):
        copy(0, j, sectors[j]).wait_recv()

    @pl.when(has_prev)
    def _():
        for j in range(n_dir):
            copy(1, j, sectors[j]).wait_recv()

    @pl.when(has_next)
    def _():
        for j in range(n_dir):
            copy(2, j, sectors[j]).wait_recv()

    def added(load):
        parts = [load(s) for s in range(n_dir)]
        total = parts[0]
        for part in parts[1:]:
            total = jax.tree.map(jnp.add, total, part)
        return total

    whole = [added(lambda s: load_tiles(full, s, q)) for q in range(3)]
    above = [added(lambda s: load_row(top, s, q, SUBS - 1)) for q in range(3)]
    below = [added(lambda s: load_row(bot, s, q, 0)) for q in range(3)]
    for out in range(2):
        ahead, behind = next_row(whole[out], below[out]), prev_row(whole[out], above[out])
        for r, row in enumerate(whole[out + 1]):
            east, west = next_col(row), prev_col(row, 0.0)
            for c in range(len(row)):
                force[out, pl.ds(r * SUBS, SUBS), pl.ds(c * LANES, LANES)] = -(
                    0.5 * (ahead[r][c] - behind[r][c]) + 0.5 * (east[c] - west[c])
                )

    for j in range(1, n_dir):
        copy(0, j, mine).wait_send()

    @pl.when(has_next)
    def _():
        for j in range(n_dir):
            copy(1, j, mine).wait_send()

    @pl.when(has_prev)
    def _():
        for j in range(n_dir):
            copy(2, j, mine).wait_send()


def geometry(n_dir, nd):
    total = n_dir * nd
    step = 2.0 * math.pi / total
    out = np.zeros((n_dir, 7, nd + 1), np.float32)
    for s in range(n_dir):
        angle = (s * nd + np.arange(nd)) * step
        index = np.arange(nd + 1) % nd if n_dir == 2 else s * nd + np.arange(nd + 1)
        phi = (index - 0.5) * step
        scale = total / (2.0 * math.pi)
        cos, sin = np.cos(angle), np.sin(angle)
        out[s, 0, :nd], out[s, 1, :nd] = cos, sin
        out[s, 2] = scale * np.sin(phi) * np.cos(phi)
        out[s, 3] = scale * np.sin(phi) ** 2
        out[s, 4] = scale * np.cos(phi) ** 2
        out[s, 5, :nd], out[s, 6, :nd] = cos * cos, sin * cos
    return out


def per_device(action, currents, land_mask, group_speed, group_ratio, bin_weight):
    nf, nd, nr, nc = action.shape
    n_pts, n_dir = lax.axis_size("pts"), lax.axis_size("dir")
    table = geometry(n_dir, nd)
    wave = np.ascontiguousarray(np.broadcast_to(table[:, :2, :nd, None], (n_dir, 2, nd, nc)))
    chunk = max(c for c in (1, 2) if nf % c == 0)
    chunks = nf // chunk
    block = max(c for c in range(1, 6) if nf % c == 0)
    sides = 1 if n_dir == 2 else 2
    vmem = pl.BlockSpec(memory_space=pltpu.VMEM)
    smem = pl.BlockSpec(memory_space=pltpu.SMEM)
    hbm = pl.BlockSpec(memory_space=pl.ANY)
    dma = pltpu.SemaphoreType.DMA
    halo = pltpu.VMEM((nf, 2, nd, nc), F32)
    a2, got, turning = pl.pallas_call(
        functools.partial(transport_kernel, n_pts, n_dir, chunk),
        out_shape=(
            jax.ShapeDtypeStruct(action.shape, F32),
            jax.ShapeDtypeStruct((sides, nf, nr, nc), F32),
            jax.ShapeDtypeStruct((nd + 1, nr, nc), F32),
        ),
        in_specs=[hbm, hbm, hbm, hbm, smem, smem],
        out_specs=(hbm, hbm, hbm),
        scratch_shapes=[
            pltpu.VMEM(action.shape, F32), pltpu.VMEM(currents.shape, F32),
            pltpu.VMEM(land_mask.shape, jnp.int32), pltpu.VMEM(wave.shape, F32),
            pltpu.VMEM((nd + 1, nr, nc), F32),
            halo, halo, halo, halo,
            pltpu.VMEM((2, SUBS, nc), F32), pltpu.VMEM((2, SUBS, nc), F32),
            pltpu.VMEM((SUBS, nc), jnp.int32), pltpu.VMEM((SUBS, nc), jnp.int32),
            pltpu.VMEM((nr, nc), F32), pltpu.VMEM((nr, nc), F32), pltpu.VMEM((nr, nc), F32),
            pltpu.VMEM((24, nc), F32), pltpu.VMEM((4, nd, nc), F32),
            pltpu.VMEM((sides, nf, nr, nc), F32),
            dma((chunks,)), dma((chunks,)), dma((4,)),
            dma((chunks,)), dma((chunks,)), dma((chunks,)),
            dma((chunks,)), dma((8,)), dma((sides, chunks)), dma((sides, chunks)),
        ],
        compiler_params=pltpu.CompilerParams(
            collective_id=0, has_side_effects=True, vmem_limit_bytes=60 * 2**20
        ),
        name="transport",
    )(action, currents, land_mask, wave, group_speed, table)
    new_action, stress = pl.pallas_call(
        refract_kernel,
        grid=(nf // block,),
        out_shape=(
            jax.ShapeDtypeStruct(action.shape, F32),
            jax.ShapeDtypeStruct((3, nr, nc), F32),
        ),
        in_specs=[
            pl.BlockSpec((block, nd, nr, nc), lambda i: (i, 0, 0, 0)),
            pl.BlockSpec((sides, block, nr, nc), lambda i: (0, i, 0, 0)),
            pl.BlockSpec((nd + 1, nr, nc), lambda i: (0, 0, 0)),
            smem, smem, smem,
        ],
        out_specs=(
            pl.BlockSpec((block, nd, nr, nc), lambda i: (i, 0, 0, 0)),
            pl.BlockSpec((3, nr, nc), lambda i: (0, 0, 0)),
        ),
        compiler_params=pltpu.CompilerParams(vmem_limit_bytes=60 * 2**20),
        name="refract",
    )(a2, got, turning, table, bin_weight, group_ratio)
    force = pl.pallas_call(
        functools.partial(force_kernel, n_pts, n_dir),
        out_shape=jax.ShapeDtypeStruct((2, nr, nc), F32),
        in_specs=[vmem],
        out_specs=vmem,
        scratch_shapes=[
            pltpu.VMEM((n_dir, 3, nr, nc), F32),
            pltpu.VMEM((n_dir, 3, SUBS, nc), F32), pltpu.VMEM((n_dir, 3, SUBS, nc), F32),
            dma((3, n_dir)), dma((3, n_dir)),
        ],
        compiler_params=pltpu.CompilerParams(
            collective_id=1, has_side_effects=True, vmem_limit_bytes=16 * 2**20
        ),
        cost_estimate=pl.CostEstimate(flops=10**6, bytes_accessed=2 * 10**7, transcendentals=0),
        name="force",
    )(stress)
    return new_action, force


def solution(mesh):
    in_specs = (P(None, "dir", "pts", None), P(None, "pts", None), P("pts", None), P(), P(), P())
    out_specs = (P(None, "dir", "pts", None), P(None, "pts", None))
    return jax.shard_map(
        per_device, mesh=mesh, in_specs=in_specs, out_specs=out_specs, check_vma=False
    )
```
